32 devices in a mesh: grp: 2 (over y), sub: 4 (over z), shot: 4 (over x, core).
Axes of the slice: x: 2, y: 2, z: 4, core: 2. Of those that a mesh axis runs over, the one named last changes fastest.
Arguments:
- model_field: float32 [32, 256, 128], P(('grp', 'sub')), parts along dimension 0, may hold values from 0.08 to 0.22
- source_index: int32 [8, 256], P(('grp', 'shot')), parts along dimension 0, may hold values from 0 to 524287
- wavelets: float32 [8, 12, 256], P(('grp', 'shot')), parts along dimension 0, may hold values from -6 to 6
- receiver_index: int32 [8, 512], P(('grp', 'shot')), parts along dimension 0, may hold values from 0 to 524287
- observed: float32 [8, 12, 512], P(('grp', 'shot')), parts along dimension 0, may hold values from -6 to 6
Outputs:
- updated_model: float32 [32, 256, 128], P(('grp', 'sub')), parts along dimension 0
- gradient: float32 [32, 256, 128], P(('grp', 'sub'), 'shot'), parts along dimension 0
The draws below stay inside these ranges and needn't reach their ends.
There are 2 independent parts, one for each index of `grp`. The reference program is written for one: setup_inputs(seed, part) draws one part's arguments, and reference() takes and returns one part's arrays. A program takes and returns all parts, laid end to end along the dimension named above; each array names one. Nothing has to cross between parts.
All inputs are finite; a program needn't handle non-finite values.
Results may differ from the reference program's by a relative error of at most 0.00002.
Values sent between devices are 32-bit elements; how exact they have to be, the bound alone decides.
A program may use at most 64 MiB of HBM per device.

```python
import jax
import jax.numpy as jnp
from jax import lax

NY = 256
NZ = 128
STEPS = 12
ITERS = 6
NSRC = 256
NREC = 512
NX = 16
SHOTS = 4


def set_ends(entries, own_key, least, high):
    extent = entries.shape
    spot = [jax.random.randint(jax.random.fold_in(own_key, axis), (), 0, extent[axis]) for axis in range(len(extent))]
    entries = entries.at[tuple(spot)].set(least)
    longest = extent.index(max(extent))
    spot[longest] = (spot[longest] + 1) % extent[longest]
    return entries.at[tuple(spot)].set(high)


def level_of(rng, shape, shards, smallest, top_value):
    level, own = 1.0, jax.random.fold_in(rng, 6)
    for dim, blocks in shards:
        heights = jnp.exp(jax.random.uniform(jax.random.fold_in(own, dim), (blocks,), jnp.float32, smallest / len(shards), top_value / len(shards)))
        level = level * jnp.repeat(heights, shape[dim] // blocks).reshape([-1 if axis == dim else 1 for axis in range(len(shape))])
    return level


def bell_draw(own_key, extent, scale, bound, cuts=(), held_as=jnp.bfloat16):
    values = jax.random.normal(own_key, extent, jnp.float32) * scale
    if len(cuts) > 0:
        values = level_of(own_key, extent, cuts, -0.22, 0.18) * values
    return jnp.clip(values, min=-bound, max=bound).astype(held_as)


def setup_inputs(seed: int = 0, part: int = 0) -> dict:
    key_of = jax.random.split(jax.random.key(seed), 6)
    part_splits = jax.random.split(jax.random.fold_in(key_of[5], part), 6)
    return {
        "model_field": jnp.clip(0.08 + 0.14 * jax.random.uniform(part_splits[0], (NX, NY, NZ), jnp.float32) ** level_of(part_splits[0], (NX, NY, NZ), ((0, 4),), -0.2, 0.2), 0.08, 0.22),
        "source_index": set_ends(jax.random.randint(part_splits[1], (SHOTS, NSRC), 0, NX * NY * NZ), jax.random.fold_in(part_splits[1], 1), 0, (NX * NY * NZ) - 1).astype(jnp.int32),
        "wavelets": bell_draw(part_splits[2], (SHOTS, STEPS, NSRC), 1.0, 6.0, ((0, 4),), jnp.float32),
        "receiver_index": set_ends(jax.random.randint(part_splits[3], (SHOTS, NREC), 0, NX * NY * NZ), jax.random.fold_in(part_splits[3], 1), 0, (NX * NY * NZ) - 1).astype(jnp.int32),
        "observed": bell_draw(part_splits[4], (SHOTS, STEPS, NREC), 1.0, 6.0, ((0, 4),), jnp.float32),
    }


near_weight = 4.0 / 3.0
far_weight = -1.0 / 12.0
centre_weight = 7.5
step_length = 0.02
tv_bound = 0.01
dual_step = 0.25
primal_step = 0.25
lower_bound = 0.08
upper_bound = 0.22
epsilon = 1e-06

def laplacian(padded):
    centre = padded[..., 2:-2, 2:-2, 2:-2]
    near = padded[..., 3:-1, 2:-2, 2:-2] + padded[..., 1:-3, 2:-2, 2:-2] + padded[..., 2:-2, 3:-1, 2:-2] + padded[..., 2:-2, 1:-3, 2:-2] + padded[..., 2:-2, 2:-2, 3:-1] + padded[..., 2:-2, 2:-2, 1:-3]
    far = padded[..., 4:, 2:-2, 2:-2] + padded[..., :-4, 2:-2, 2:-2] + padded[..., 2:-2, 4:, 2:-2] + padded[..., 2:-2, :-4, 2:-2] + padded[..., 2:-2, 2:-2, 4:] + padded[..., 2:-2, 2:-2, :-4]
    return near_weight * near + far_weight * far - centre_weight * centre

def forward_diff(field, along):
    size = field.shape[along]
    diff = lax.slice_in_dim(field, 1, size, axis=along) - lax.slice_in_dim(field, 0, size - 1, axis=along)
    return jnp.concatenate([diff, jnp.zeros_like(lax.slice_in_dim(field, 0, 1, axis=along))], along)

def backward_diff(dual, along):
    size = dual.shape[along]
    earlier = jnp.concatenate([jnp.zeros_like(lax.slice_in_dim(dual, 0, 1, axis=along)), lax.slice_in_dim(dual, 0, size - 1, axis=along)], along)
    return earlier - dual

def reference(model_field, source_index, wavelets, receiver_index, observed):
    shape = model_field.shape

    def one_shot(pieces):
        sources, wave_all, receivers, seen = pieces
        blank = jnp.zeros(shape, jnp.float32)

        def forward(state, wave_now):
            earlier, current = state
            stored = laplacian(jnp.pad(current, 2))
            following = 2.0 * current - earlier + model_field * stored
            flat = following.reshape(-1).at[sources].add(wave_now)
            return ((current, flat.reshape(shape)), (stored, flat[receivers]))
        _, (laps, record) = lax.scan(forward, (blank, blank), wave_all)
        misfit = record - seen

        def backward(state, inputs):
            earlier, current, gradient_sum = state
            stored, misfit_now = inputs
            following = 2.0 * current - earlier + model_field * laplacian(jnp.pad(current, 2))
            following = following.reshape(-1).at[receivers].add(misfit_now).reshape(shape)
            return ((current, following, gradient_sum + following * stored), None)
        (_, _, gradient_sum), _ = lax.scan(backward, (blank, blank, blank), (laps[::-1], misfit[::-1]))
        return gradient_sum
    per_shot = lax.map(one_shot, (source_index, wavelets, receiver_index, observed))
    gradient = lax.optimization_barrier(jnp.sum(per_shot, 0))
    grad_scale = jnp.sqrt(jnp.sum(gradient * gradient) / gradient.size + epsilon)
    target = model_field - step_length * (gradient / grad_scale)
    field = jnp.clip(target, lower_bound, upper_bound)
    extrap = field
    duals = [jnp.zeros_like(field) for along in range(3)]
    for iteration in range(ITERS):
        duals = [jnp.clip(duals[along] + dual_step * forward_diff(extrap, along), -tv_bound, tv_bound) for along in range(3)]
        adjoint = backward_diff(duals[0], 0) + backward_diff(duals[1], 1) + backward_diff(duals[2], 2)
        following = jnp.clip((field - primal_step * adjoint + primal_step * target) / (1.0 + primal_step), lower_bound, upper_bound)
        extrap = 2.0 * following - field
        field = following
    return (field, gradient)
```

```python
import functools

import jax
import jax.numpy as jnp
from jax import lax
from jax.experimental import pallas as pl
from jax.experimental.pallas import tpu as pltpu
from jax.sharding import PartitionSpec as P

ITERS = 6

near_weight = 4.0 / 3.0
far_weight = -1.0 / 12.0
centre_weight = 7.5
step_length = 0.02
tv_bound = 0.01
dual_step = 0.25
primal_step = 0.25
lower_bound = 0.08
upper_bound = 0.22
epsilon = 1e-06

VMEM_LIMIT = 58 * 1024 * 1024


def from_behind(value, axis, steps):
    count = lax.axis_size(axis)
    initial, last = (max(0, -steps), min(count, count - steps))
    return lax.ppermute(value, axis, [(source, source + steps) for source in range(initial, last)])


def forward_part(field, along, upper, last_owner):
    size = field.shape[along]
    first_row = lax.slice_in_dim(field, 0, 1, axis=along)
    remainder = lax.slice_in_dim(field, 1, size, axis=along)
    beyond = jnp.zeros_like(first_row) if upper is None else upper(first_row)
    difference = jnp.concatenate([remainder, beyond], along) - field
    row_index = lax.broadcasted_iota(jnp.int32, field.shape, along)
    return jnp.where(jnp.logical_and(row_index == size - 1, last_owner), 0.0, difference)


def backward_part(dual, along, lower):
    size = dual.shape[along]
    last_row = lax.slice_in_dim(dual, size - 1, size, axis=along)
    before = jnp.zeros_like(last_row) if lower is None else lower(last_row)
    earlier = jnp.concatenate([before, lax.slice_in_dim(dual, 0, size - 1, axis=along)], along)
    return earlier - dual


def project(target, upper_x, lower_x, last_x):
    field = jnp.clip(target, lower_bound, upper_bound)
    extrap = field
    duals = [jnp.zeros_like(field) for along in range(3)]
    for iteration in range(ITERS):
        duals = [
            jnp.clip(
                duals[0] + dual_step * forward_part(extrap, 0, upper_x, last_x), -tv_bound, tv_bound
            ),
            jnp.clip(
                duals[1] + dual_step * forward_part(extrap, 1, None, True), -tv_bound, tv_bound
            ),
            jnp.clip(
                duals[2] + dual_step * forward_part(extrap, 2, None, True), -tv_bound, tv_bound
            ),
        ]
        adjoint = (
            backward_part(duals[0], 0, lower_x)
            + backward_part(duals[1], 1, None)
            + backward_part(duals[2], 2, None)
        )
        following = jnp.clip(
            (field - primal_step * adjoint + primal_step * target) / (1.0 + primal_step),
            lower_bound,
            upper_bound,
        )
        extrap = 2.0 * following - field
        field = following
    return field


def two_pieces(value):
    high = value.astype(jnp.bfloat16)
    low = (value - high.astype(jnp.float32)).astype(jnp.bfloat16)
    return high, low


def one_hot_rows(cells, layers, rows, first_row, height, width):
    lines = cells // width
    layer = lines // height
    row = lines - layer * height - first_row
    inside = jnp.logical_and(row >= 0, row < rows)
    return jnp.where(inside, layer * rows + row, -1)


def advance(model, current, earlier, injected, column, extent, keep, accumulate):
    layers, rows, width = extent
    lane = lax.broadcasted_iota(jnp.int32, (1, width), 1)
    weights = [
        (1, jnp.where(lane >= 1, near_weight, 0.0)),
        (width - 1, jnp.where(lane < width - 1, near_weight, 0.0)),
        (2, jnp.where(lane >= 2, far_weight, 0.0)),
        (width - 2, jnp.where(lane < width - 2, far_weight, 0.0)),
    ]

    def layer_step(layer, carry):
        centre = current[layer + 2]
        near = current[layer + 1] + current[layer + 3]
        far = current[layer] + current[layer + 4]
        near = near + (pltpu.roll(centre, 1, 0) + pltpu.roll(centre, rows - 1, 0))
        far = far + (pltpu.roll(centre, 2, 0) + pltpu.roll(centre, rows - 2, 0))
        lap = near_weight * near + far_weight * far - centre_weight * centre
        for shift, weight in weights:
            lap = lap + weight * pltpu.roll(centre, shift, 1)
        start = layer * rows if isinstance(layer, int) else pl.multiple_of(layer * rows, 8)
        following = 2.0 * centre - earlier[layer + 2] + model[layer] * lap
        following = following + injected[pl.ds(start, rows), pl.ds(column, width)]
        earlier[layer + 2] = following
        if keep is not None:
            keep(layer, lap)
        if accumulate is not None:
            accumulate(layer, following)
        return carry

    if layers <= 16:
        for layer in range(layers):
            layer_step(layer, 0)
    else:
        lax.fori_loop(0, layers, layer_step, 0)


def fill_one_hot(target, positions):
    step = 256
    for begin in range(0, target.shape[0], step):
        grid_row = lax.broadcasted_iota(jnp.int32, (step, target.shape[1]), 0) + begin
        target[begin : begin + step, :] = jnp.where(grid_row == positions, 1.0, 0.0).astype(jnp.bfloat16)


def inject(spread, values, injected):
    high, low = two_pieces(values)
    injected[...] = jnp.dot(spread[...], high, preferred_element_type=jnp.float32) + jnp.dot(
        spread[...], low, preferred_element_type=jnp.float32
    )


def forward_kernel(
    geometry, model, sources, receivers_column, values, laps, record, first, second, injected, spread, pick
):
    layers, rows, own, halo, height, width = geometry
    start_row = lax.axis_index("sub") * own
    fill_one_hot(spread, one_hot_rows(sources[...], layers, rows, start_row - halo, height, width))
    first[...] = jnp.zeros_like(first)
    second[...] = jnp.zeros_like(second)
    column = receivers_column[...]
    owned = one_hot_rows(column, layers, own, start_row, height, width)
    cells = layers * own
    for begin in range(0, cells, 256):
        numbers = lax.broadcasted_iota(jnp.int32, (column.shape[0], 256), 1) + begin
        pick[:, begin : begin + 256] = jnp.where(numbers == owned, 1.0, 0.0).astype(jnp.bfloat16)
    lane = lax.broadcasted_iota(jnp.int32, (column.shape[0], width), 1)
    mask = jnp.where(lane == column - (column // width) * width, 1.0, 0.0)
    ones = jnp.ones((8, width), jnp.bfloat16)

    def sample(field, step):
        values = field[2 : 2 + layers, halo : halo + own, :].reshape(cells, width)
        found = [
            jnp.dot(pick[...], piece, preferred_element_type=jnp.float32)
            for piece in two_pieces(values)
        ]
        pieces = [piece * mask for piece in found]
        total = jnp.zeros((8, column.shape[0]), jnp.float32)
        for piece in pieces:
            total = total + lax.dot_general(
                ones, piece.astype(jnp.bfloat16), (((1,), (1,)), ((), ())), preferred_element_type=jnp.float32
            )
        record[pl.ds(step, 1), :] = total[0:1]

    def pair(number, carry):
        inject(spread, values[number], injected)
        for half, (current, earlier) in enumerate(((second, first), (first, second))):
            step = number * 2 + half

            def keep(layer, lap):
                laps[step, layer] = lap[halo : halo + own]

            advance(model, current, earlier, injected, half * width, (layers, rows, width), keep, None)
            sample(earlier, step)
        return carry

    lax.fori_loop(0, values.shape[0], pair, 0)


def backward_kernel(geometry, model, receivers, values, laps, gradient, first, second, injected, spread):
    layers, rows, own, halo, height, width = geometry
    start_row = lax.axis_index("sub") * own
    fill_one_hot(spread, one_hot_rows(receivers[...], layers, rows, start_row - halo, height, width))
    first[...] = jnp.zeros_like(first)
    second[...] = jnp.zeros_like(second)
    gradient[...] = jnp.zeros_like(gradient)
    steps = laps.shape[0]

    def pair(number, carry):
        inject(spread, values[number], injected)
        for half, (current, earlier) in enumerate(((second, first), (first, second))):
            step = number * 2 + half

            def accumulate(layer, following):
                gradient[layer] += following[halo : halo + own] * laps[steps - 1 - step, layer]

            advance(
                model, current, earlier, injected, half * width, (layers, rows, width), None, accumulate
            )
        return carry

    lax.fori_loop(0, values.shape[0], pair, 0)


def spread_values(amounts, cells, width):
    steps, points = amounts.shape
    pairs = amounts.reshape(steps // 2, 2, points)
    lane = cells % width
    hot = (lane[:, None] == jnp.arange(width, dtype=jnp.int32)[None]).astype(jnp.float32)
    spread = [pairs[:, half, :, None] * hot[None] for half in range(2)]
    return jnp.concatenate(spread, axis=2)


def per_device(model_field, source_index, wavelets, receiver_index, observed):
    slab, height, width = model_field.shape
    subs = lax.axis_size("sub")
    layers = slab * subs
    own = height // subs
    steps = wavelets.shape[1]
    halo = 2 * steps
    rows = own + 2 * halo
    geometry = (layers, rows, own, halo, height, width)

    wide = jnp.pad(model_field, ((0, 0), (halo, halo), (0, 0)))
    parts = jnp.stack([wide[:, j * own : j * own + rows] for j in range(subs)])
    model = lax.all_to_all(parts, "sub", 0, 0).reshape(layers, rows, width)

    vmem = pl.BlockSpec(memory_space=pltpu.VMEM)
    field = pltpu.VMEM((layers + 4, rows, width), jnp.float32)
    injected = pltpu.VMEM((layers * rows, 2 * width), jnp.float32)
    params = pltpu.CompilerParams(vmem_limit_bytes=VMEM_LIMIT)
    sources, receivers = source_index, receiver_index
    values = spread_values(wavelets[0], sources[0], width)
    laps, record = pl.pallas_call(
        functools.partial(forward_kernel, geometry),
        out_shape=(
            jax.ShapeDtypeStruct((steps, layers, own, width), jnp.float32),
            jax.ShapeDtypeStruct((steps, receivers.shape[1]), jnp.float32),
        ),
        in_specs=[vmem] * 4,
        out_specs=(vmem, vmem),
        scratch_shapes=[
            field,
            field,
            injected,
            pltpu.VMEM((layers * rows, sources.shape[1]), jnp.bfloat16),
            pltpu.VMEM((receivers.shape[1], layers * own), jnp.bfloat16),
        ],
        compiler_params=params,
    )(model, sources, receivers.reshape(-1, 1), values)
    misfit = lax.psum(record, "sub") - observed[0]
    values = spread_values(misfit[::-1], receivers[0], width)
    part_gradient = pl.pallas_call(
        functools.partial(backward_kernel, geometry),
        out_shape=jax.ShapeDtypeStruct((layers, own, width), jnp.float32),
        in_specs=[vmem] * 4,
        out_specs=vmem,
        scratch_shapes=[
            field,
            field,
            injected,
            pltpu.VMEM((layers * rows, receivers.shape[1]), jnp.bfloat16),
        ],
        compiler_params=params,
    )(model, receivers, values, laps)

    local_gradient = lax.all_to_all(part_gradient.reshape(subs, slab, own, width), "sub", 0, 0)
    local_gradient = jnp.swapaxes(local_gradient, 0, 1).reshape(slab, height, width)
    last_x = lax.axis_index("sub") == subs - 1
    slab_gradient = lax.psum(local_gradient, "shot")
    square_sum = lax.psum(jnp.sum(slab_gradient * slab_gradient), "sub")
    grad_scale = jnp.sqrt(square_sum / (slab * height * width * subs) + epsilon)
    target = model_field - step_length * (slab_gradient / grad_scale)

    def slab_upper(layer):
        return from_behind(layer, "sub", -1)

    def slab_lower(layer):
        return from_behind(layer, "sub", 1)

    updated_model = project(target, slab_upper, slab_lower, last_x)
    brick_rows = height // lax.axis_size("shot")
    gradient = lax.dynamic_slice_in_dim(
        slab_gradient, lax.axis_index("shot") * brick_rows, brick_rows, 1
    )
    return (updated_model, gradient)


def solution(mesh):
    placed = (
        P(("grp", "sub"), None, None),
        P(("grp", "shot"), None),
        P(("grp", "shot"), None, None),
        P(("grp", "shot"), None),
        P(("grp", "shot"), None, None),
    )
    return jax.shard_map(
        per_device,
        mesh=mesh,
        in_specs=placed,
        out_specs=(P(("grp", "sub"), None, None), P(("grp", "sub"), "shot", None)),
        check_vma=False,
    )
```

```python
import functools

import jax
import jax.numpy as jnp
from jax import lax
from jax.experimental import pallas as pl
from jax.experimental.pallas import tpu as pltpu
from jax.sharding import PartitionSpec as P

ITERS = 6

near_weight = 4.0 / 3.0
far_weight = -1.0 / 12.0
centre_weight = 7.5
step_length = 0.02
tv_bound = 0.01
dual_step = 0.25
primal_step = 0.25
lower_bound = 0.08
upper_bound = 0.22
epsilon = 1e-06

VMEM_LIMIT = 58 * 1024 * 1024


def from_behind(value, axis, steps):
    count = lax.axis_size(axis)
    initial, last = (max(0, -steps), min(count, count - steps))
    return lax.ppermute(value, axis, [(source, source + steps) for source in range(initial, last)])


def forward_part(field, along, upper, last_owner):
    size = field.shape[along]
    first_row = lax.slice_in_dim(field, 0, 1, axis=along)
    remainder = lax.slice_in_dim(field, 1, size, axis=along)
    beyond = jnp.zeros_like(first_row) if upper is None else upper(first_row)
    difference = jnp.concatenate([remainder, beyond], along) - field
    row_index = lax.broadcasted_iota(jnp.int32, field.shape, along)
    return jnp.where(jnp.logical_and(row_index == size - 1, last_owner), 0.0, difference)


def backward_part(dual, along, lower):
    size = dual.shape[along]
    last_row = lax.slice_in_dim(dual, size - 1, size, axis=along)
    before = jnp.zeros_like(last_row) if lower is None else lower(last_row)
    earlier = jnp.concatenate([before, lax.slice_in_dim(dual, 0, size - 1, axis=along)], along)
    return earlier - dual


def project(target, upper_x, lower_x, last_x):
    field = jnp.clip(target, lower_bound, upper_bound)
    extrap = field
    duals = [jnp.zeros_like(field) for along in range(3)]
    for iteration in range(ITERS):
        duals = [
            jnp.clip(
                duals[0] + dual_step * forward_part(extrap, 0, upper_x, last_x), -tv_bound, tv_bound
            ),
            jnp.clip(
                duals[1] + dual_step * forward_part(extrap, 1, None, True), -tv_bound, tv_bound
            ),
            jnp.clip(
                duals[2] + dual_step * forward_part(extrap, 2, None, True), -tv_bound, tv_bound
            ),
        ]
        adjoint = (
            backward_part(duals[0], 0, lower_x)
            + backward_part(duals[1], 1, None)
            + backward_part(duals[2], 2, None)
        )
        following = jnp.clip(
            (field - primal_step * adjoint + primal_step * target) / (1.0 + primal_step),
            lower_bound,
            upper_bound,
        )
        extrap = 2.0 * following - field
        field = following
    return field


def three_pieces(value):
    pieces = []
    for _ in range(2):
        piece = value.astype(jnp.bfloat16)
        pieces.append(piece)
        value = value - piece.astype(jnp.float32)
    return pieces + [value.astype(jnp.bfloat16)]


def one_hot_rows(cells, layers, rows, first_row, height, width):
    lines = cells // width
    layer = lines // height
    row = lines - layer * height - first_row
    inside = jnp.logical_and(row >= 0, row < rows)
    return jnp.where(inside, layer * rows + row, -1)


def advance(model, current, earlier, injected, column, extent, keep, accumulate):
    layers, rows, width = extent
    lane = lax.broadcasted_iota(jnp.int32, (1, width), 1)
    weights = [
        (1, jnp.where(lane >= 1, near_weight, 0.0)),
        (width - 1, jnp.where(lane < width - 1, near_weight, 0.0)),
        (2, jnp.where(lane >= 2, far_weight, 0.0)),
        (width - 2, jnp.where(lane < width - 2, far_weight, 0.0)),
    ]

    def layer_step(layer, carry):
        centre = current[layer + 2]
        near = current[layer + 1] + current[layer + 3]
        far = current[layer] + current[layer + 4]
        near = near + (pltpu.roll(centre, 1, 0) + pltpu.roll(centre, rows - 1, 0))
        far = far + (pltpu.roll(centre, 2, 0) + pltpu.roll(centre, rows - 2, 0))
        lap = near_weight * near + far_weight * far - centre_weight * centre
        for shift, weight in weights:
            lap = lap + weight * pltpu.roll(centre, shift, 1)
        start = layer * rows if isinstance(layer, int) else pl.multiple_of(layer * rows, 8)
        following = 2.0 * centre - earlier[layer + 2] + model[layer] * lap
        following = following + injected[pl.ds(start, rows), pl.ds(column, width)]
        earlier[layer + 2] = following
        if keep is not None:
            keep(layer, lap)
        if accumulate is not None:
            accumulate(layer, following)
        return carry

    if layers <= 16:
        for layer in range(layers):
            layer_step(layer, 0)
    else:
        lax.fori_loop(0, layers, layer_step, 0)


def fill_one_hot(target, positions):
    step = 256
    for begin in range(0, target.shape[0], step):
        grid_row = lax.broadcasted_iota(jnp.int32, (step, target.shape[1]), 0) + begin
        target[begin : begin + step, :] = jnp.where(grid_row == positions, 1.0, 0.0).astype(jnp.bfloat16)


def inject(spread, values, injected):
    high, middle, low = [
        jnp.dot(spread[...], piece, preferred_element_type=jnp.float32) for piece in three_pieces(values)
    ]
    injected[...] = high + (middle + low)


def forward_kernel(
    geometry, model, sources, receivers_column, values, laps, record, first, second, injected, spread, pick
):
    layers, rows, own, halo, height, width = geometry
    start_row = lax.axis_index("sub") * own
    fill_one_hot(spread, one_hot_rows(sources[...], layers, rows, start_row - halo, height, width))
    first[...] = jnp.zeros_like(first)
    second[...] = jnp.zeros_like(second)
    column = receivers_column[...]
    owned = one_hot_rows(column, layers, own, start_row, height, width)
    cells = layers * own
    for begin in range(0, cells, 256):
        numbers = lax.broadcasted_iota(jnp.int32, (column.shape[0], 256), 1) + begin
        pick[:, begin : begin + 256] = jnp.where(numbers == owned, 1.0, 0.0).astype(jnp.bfloat16)
    lane = lax.broadcasted_iota(jnp.int32, (column.shape[0], width), 1)
    mask = jnp.where(lane == column - (column // width) * width, 1.0, 0.0)
    ones = jnp.ones((8, width), jnp.bfloat16)

    def sample(field, step):
        values = field[2 : 2 + layers, halo : halo + own, :].reshape(cells, width)
        found = [
            jnp.dot(pick[...], piece, preferred_element_type=jnp.float32)
            for piece in three_pieces(values)
        ]
        pieces = [piece * mask for piece in found]
        total = jnp.zeros((8, column.shape[0]), jnp.float32)
        for piece in pieces:
            total = total + lax.dot_general(
                ones, piece.astype(jnp.bfloat16), (((1,), (1,)), ((), ())), preferred_element_type=jnp.float32
            )
        record[pl.ds(step, 1), :] = total[0:1]

    def pair(number, carry):
        inject(spread, values[number], injected)
        for half, (current, earlier) in enumerate(((second, first), (first, second))):
            step = number * 2 + half

            def keep(layer, lap):
                laps[step, layer] = lap[halo : halo + own]

            advance(model, current, earlier, injected, half * width, (layers, rows, width), keep, None)
            sample(earlier, step)
        return carry

    lax.fori_loop(0, values.shape[0], pair, 0)


def backward_kernel(geometry, model, receivers, values, laps, gradient, first, second, injected, spread):
    layers, rows, own, halo, height, width = geometry
    start_row = lax.axis_index("sub") * own
    fill_one_hot(spread, one_hot_rows(receivers[...], layers, rows, start_row - halo, height, width))
    first[...] = jnp.zeros_like(first)
    second[...] = jnp.zeros_like(second)
    gradient[...] = jnp.zeros_like(gradient)
    steps = laps.shape[0]

    def pair(number, carry):
        inject(spread, values[number], injected)
        for half, (current, earlier) in enumerate(((second, first), (first, second))):
            step = number * 2 + half

            def accumulate(layer, following):
                gradient[layer] += following[halo : halo + own] * laps[steps - 1 - step, layer]

            advance(
                model, current, earlier, injected, half * width, (layers, rows, width), None, accumulate
            )
        return carry

    lax.fori_loop(0, values.shape[0], pair, 0)


def spread_values(amounts, cells, width):
    steps, points = amounts.shape
    pairs = amounts.reshape(steps // 2, 2, points)
    lane = cells % width
    hot = (lane[:, None] == jnp.arange(width, dtype=jnp.int32)[None]).astype(jnp.float32)
    spread = [pairs[:, half, :, None] * hot[None] for half in range(2)]
    return jnp.concatenate(spread, axis=2)


def peers_barrier(peers):
    barrier = pltpu.get_barrier_semaphore()
    for peer in peers:
        pl.semaphore_signal(barrier, inc=1, device_id=peer, device_id_type=pl.DeviceIdType.MESH)
    pl.semaphore_wait(barrier, len(peers))


def remote(source, target, send, receive, peer):
    return pltpu.make_async_remote_copy(
        src_ref=source,
        dst_ref=target,
        send_sem=send,
        recv_sem=receive,
        device_id=peer,
        device_id_type=pl.DeviceIdType.MESH,
    )


def model_kernel(subs, own, wide, model, send, receive, local):
    me = lax.axis_index("sub")
    slab = wide.shape[0]
    rows = model.shape[1]
    peers = [{"sub": lax.rem(me + d, subs)} for d in range(1, subs)]
    peers_barrier(peers)
    place = model.at[pl.ds(me * slab, slab)]

    def rows_of(sub):
        return wide.at[:, pl.ds(pl.multiple_of(sub * own, 8), rows), :]

    copies = []
    for d, peer in enumerate(peers):
        copy = remote(rows_of(peer["sub"]), place, send.at[d], receive.at[d], peer)
        copy.start()
        copies.append(copy)
    mine = pltpu.make_async_copy(rows_of(me), place, local)
    mine.start()
    mine.wait()
    for d, copy in enumerate(copies):
        copy.wait_send()
        origin = lax.rem(me + subs - d - 1, subs)
        remote(
            rows_of(me), model.at[pl.ds(origin * slab, slab)], send.at[d], receive.at[d], peers[d]
        ).wait_recv()


def record_kernel(subs, record, observed, misfit, slots, send, receive):
    me = lax.axis_index("sub")
    peers = [{"sub": lax.rem(me + d, subs)} for d in range(1, subs)]
    peers_barrier(peers)
    copies = []
    for d, peer in enumerate(peers):
        copy = remote(record, slots.at[d], send.at[d], receive.at[d], peer)
        copy.start()
        copies.append(copy)
    total = record[...]
    for d, copy in enumerate(copies):
        copy.wait()
        total = total + slots[d]
    misfit[...] = total - observed[...]


def update_kernel(
    geometry, subs, shots, part, model, updated, gradient,
    near, own_model, strip, squares, arrived_squares, above, below,
    field, extrap, target, dual_x, dual_y, dual_z, strip_out, slab_out, brick,
    local, send_sum, get_sum, send_square, get_square, send_halo, get_halo,
    send_brick, get_brick, send_slab, get_slab, send_on, get_on,
):
    layers, rows, own, halo, height, width = geometry
    slab = layers // subs
    lines = own // shots
    sub, shot = lax.axis_index("sub"), lax.axis_index("shot")

    def at(d_sub, d_shot):
        return {"sub": lax.rem(sub + d_sub, subs), "shot": lax.rem(shot + d_shot, shots)}

    def tiles(first):
        return pl.ds(pl.multiple_of(first, 8), lines)

    group = [(a, b) for a in range(subs) for b in range(shots) if (a, b) != (0, 0)]
    fetch = pltpu.make_async_copy(
        model.at[:, pl.ds(pl.multiple_of(halo + shot * lines - 8, 8), lines + 16), :], own_model, local
    )
    fetch.start()
    peers_barrier([at(a, b) for a, b in group])

    copies = []
    for d in range(1, shots):
        peer = at(0, d)
        copy = remote(
            part.at[:, tiles(peer["shot"] * lines), :], near.at[d - 1], send_sum.at[d - 1], get_sum.at[d - 1], peer
        )
        copy.start()
        copies.append(copy)
    for copy in copies:
        copy.wait()
    square = jnp.zeros((8, width), jnp.float32)
    for layer in range(layers):
        value = part[layer, tiles(shot * lines), :]
        for d in range(shots - 1):
            value = value + near[d, layer]
        strip[layer] = value
        for begin in range(0, lines, 8):
            square = square + value[begin : begin + 8] * value[begin : begin + 8]
    squares[...] = square

    number = sub * shots + shot
    count = subs * shots
    halos = []
    for way, (step, begin, place) in enumerate(((1, lines - 8, above), (count - 1, 0, below))):
        other = lax.rem(number + step, count)
        peer = {"sub": other // shots, "shot": lax.rem(other, shots)}
        copy = remote(
            strip.at[:, pl.ds(begin, 8), :], place, send_halo.at[way], get_halo.at[way], peer
        )
        copy.start()
        halos.append(copy)
    sums = []
    for slot, (a, b) in enumerate(group):
        copy = remote(squares, arrived_squares.at[slot], send_square.at[slot], get_square.at[slot], at(a, b))
        copy.start()
        sums.append(copy)
    here = sub == shot
    bricks = []
    for d in range(subs):
        peer = {"sub": lax.rem(sub + d, subs), "shot": sub}
        bricks.append(
            remote(
                strip.at[pl.ds(peer["sub"] * slab, slab)],
                brick.at[:, tiles(shot * lines), :],
                send_brick.at[d],
                get_brick.at[shot],
                peer,
            )
        )
    for copy in bricks[1:]:
        copy.start()

    @pl.when(jnp.logical_not(here))
    def _():
        bricks[0].start()

    @pl.when(here)
    def _():
        brick[:, tiles(shot * lines), :] = strip[pl.ds(sub * slab, slab)]

    for copy in sums + halos:
        copy.wait()
    total = squares[...]
    for slot in range(len(group)):
        total = total + arrived_squares[slot]
    total = jnp.sum(total, axis=(0, 1), keepdims=True)
    factor = step_length / jnp.sqrt(total / (layers * height * width) + epsilon)
    fetch.wait()

    tall = lines + 16
    for layer in range(layers):
        value = jnp.concatenate([above[layer], strip[layer], below[layer]], 0)
        value = own_model[layer] - factor * value
        target[layer] = value
        value = jnp.clip(value, lower_bound, upper_bound)
        field[layer] = value
        extrap[layer] = value
        for dual in (dual_x, dual_y, dual_z):
            dual[layer] = jnp.zeros((tall, width), jnp.float32)
    grid_row = lax.broadcasted_iota(jnp.int32, (tall, 1), 0) + (number * lines - 8)
    row_weight = jnp.where(jnp.logical_and(grid_row >= 0, grid_row < height - 1), dual_step, 0.0)
    lane = lax.broadcasted_iota(jnp.int32, (1, width), 1)
    lane_weight = jnp.where(lane < width - 1, dual_step, 0.0)

    def iteration(turn, carry):
        before = jnp.zeros((tall, width), jnp.float32)
        for layer in range(layers):
            value = extrap[layer]
            along_x = before
            if layer < layers - 1:
                along_x = dual_x[layer] + dual_step * (extrap[layer + 1] - value)
                along_x = jnp.clip(along_x, -tv_bound, tv_bound)
                dual_x[layer] = along_x
            else:
                along_x = jnp.zeros_like(before)
            along_y = dual_y[layer] + row_weight * (pltpu.roll(value, tall - 1, 0) - value)
            along_y = jnp.clip(along_y, -tv_bound, tv_bound)
            dual_y[layer] = along_y
            along_z = dual_z[layer] + lane_weight * (pltpu.roll(value, width - 1, 1) - value)
            along_z = jnp.clip(along_z, -tv_bound, tv_bound)
            dual_z[layer] = along_z
            adjoint = (
                (before - along_x)
                + (pltpu.roll(along_y, 1, 0) - along_y)
                + (pltpu.roll(along_z, 1, 1) - along_z)
            )
            old = field[layer]
            new = (old - primal_step * adjoint + primal_step * target[layer]) * (1.0 / (1.0 + primal_step))
            new = jnp.clip(new, lower_bound, upper_bound)
            extrap[layer] = 2.0 * new - old
            field[layer] = new
            before = along_x
        return carry

    lax.fori_loop(0, ITERS, iteration, 0)
    for layer in range(layers):
        strip_out[layer] = field[layer, 8 : 8 + lines]

    def place(d_sub, d_shot):
        origin_sub = lax.rem(sub + subs - d_sub, subs)
        origin_shot = lax.rem(shot + shots - d_shot, shots)
        return slab_out.at[:, tiles(origin_sub * own + origin_shot * lines), :]

    slabs = []
    for d in range(1, subs):
        peer = at(d, 0)
        copy = remote(
            strip_out.at[pl.ds(peer["sub"] * slab, slab)], place(0, 0), send_slab.at[d - 1], get_slab.at[d - 1], peer
        )
        copy.start()
        slabs.append(copy)
    slab_out[:, tiles(sub * own + shot * lines), :] = strip_out[pl.ds(sub * slab, slab)]
    onward = []
    for d in range(subs):
        if d > 0:
            remote(
                strip_out.at[pl.ds(sub * slab, slab)], place(d, 0), send_slab.at[d - 1], get_slab.at[d - 1], at(d, 0)
            ).wait_recv()
        for e in range(1, shots):
            copy = remote(place(d, 0), place(d, 0), send_on.at[d, e - 1], get_on.at[d, e - 1], at(0, e))
            copy.start()
            onward.append((d, e, copy))
    for copy in bricks[1:]:
        copy.wait_send()

    @pl.when(jnp.logical_not(here))
    def _():
        bricks[0].wait_send()

    for origin in range(shots):

        @pl.when(jnp.logical_not(jnp.logical_and(here, shot == origin)))
        def _():
            remote(
                strip.at[pl.ds(0, slab)],
                brick.at[:, pl.ds(origin * lines, lines), :],
                send_brick.at[0],
                get_brick.at[origin],
                at(1, 0),
            ).wait_recv()

    gradient[...] = brick[...]
    for copy in slabs:
        copy.wait_send()
    for d, e, copy in onward:
        copy.wait_send()
        remote(place(d, e), place(d, e), send_on.at[d, e - 1], get_on.at[d, e - 1], at(0, e)).wait_recv()
    updated[...] = slab_out[...]


def update_by_strips(part, model, geometry, subs, shots, params):
    layers, rows, own, halo, height, width = geometry
    slab, lines = layers // subs, own // shots
    tall = lines + 16
    vmem = pl.BlockSpec(memory_space=pltpu.VMEM)

    def space(*shape):
        return pltpu.VMEM(shape, jnp.float32)

    def sems(*shape):
        return pltpu.SemaphoreType.DMA(shape)

    others = subs * shots - 1
    return pl.pallas_call(
        functools.partial(update_kernel, geometry, subs, shots),
        out_shape=(
            jax.ShapeDtypeStruct((slab, height, width), jnp.float32),
            jax.ShapeDtypeStruct((slab, own, width), jnp.float32),
        ),
        in_specs=[vmem, pl.BlockSpec(memory_space=pl.ANY)],
        out_specs=(vmem, vmem),
        scratch_shapes=[
            space(shots - 1, layers, lines, width),
            space(layers, tall, width),
            space(layers, lines, width),
            space(8, width),
            space(others, 8, width),
            space(layers, 8, width),
            space(layers, 8, width),
        ]
        + [space(layers, tall, width)] * 6
        + [space(layers, lines, width), space(slab, height, width), space(slab, own, width)]
        + [pltpu.SemaphoreType.DMA]
        + [sems(shots - 1)] * 2
        + [sems(others)] * 2
        + [sems(2)] * 2
        + [sems(subs), sems(shots)]
        + [sems(subs - 1)] * 2
        + [sems(subs, shots - 1)] * 2,
        compiler_params=params(2),
    )(part, model)


def update_by_slabs(part, model_field, geometry, subs):
    layers, rows, own, halo, height, width = geometry
    slab = layers // subs
    local_gradient = lax.all_to_all(part.reshape(subs, slab, own, width), "sub", 0, 0)
    local_gradient = jnp.swapaxes(local_gradient, 0, 1).reshape(slab, height, width)
    last_x = lax.axis_index("sub") == subs - 1
    slab_gradient = lax.psum(local_gradient, "shot")
    square_sum = lax.psum(jnp.sum(slab_gradient * slab_gradient), "sub")
    grad_scale = jnp.sqrt(square_sum / (layers * height * width) + epsilon)
    target = model_field - step_length * (slab_gradient / grad_scale)

    def slab_upper(layer):
        return from_behind(layer, "sub", -1)

    def slab_lower(layer):
        return from_behind(layer, "sub", 1)

    updated_model = project(target, slab_upper, slab_lower, last_x)
    brick_rows = height // lax.axis_size("shot")
    gradient = lax.dynamic_slice_in_dim(
        slab_gradient, lax.axis_index("shot") * brick_rows, brick_rows, 1
    )
    return (updated_model, gradient)


def per_device(model_field, source_index, wavelets, receiver_index, observed):
    slab, height, width = model_field.shape
    subs = lax.axis_size("sub")
    layers = slab * subs
    own = height // subs
    steps = wavelets.shape[1]
    halo = 2 * steps
    rows = own + 2 * halo
    geometry = (layers, rows, own, halo, height, width)

    wide = jnp.pad(model_field, ((0, 0), (halo, halo), (0, 0)))
    def remote_params(number):
        return pltpu.CompilerParams(
            collective_id=number, has_side_effects=True, vmem_limit_bytes=VMEM_LIMIT
        )

    vmem = pl.BlockSpec(memory_space=pltpu.VMEM)
    model = pl.pallas_call(
        functools.partial(model_kernel, subs, own),
        out_shape=jax.ShapeDtypeStruct((layers, rows, width), jnp.float32),
        in_specs=[vmem],
        out_specs=vmem,
        scratch_shapes=[pltpu.SemaphoreType.DMA((subs - 1,))] * 2 + [pltpu.SemaphoreType.DMA],
        compiler_params=remote_params(0),
    )(wide)

    field = pltpu.VMEM((layers + 4, rows, width), jnp.float32)
    injected = pltpu.VMEM((layers * rows, 2 * width), jnp.float32)
    params = pltpu.CompilerParams(vmem_limit_bytes=VMEM_LIMIT)
    sources, receivers = source_index, receiver_index
    values = spread_values(wavelets[0], sources[0], width)
    laps, record = pl.pallas_call(
        functools.partial(forward_kernel, geometry),
        out_shape=(
            jax.ShapeDtypeStruct((steps, layers, own, width), jnp.float32),
            jax.ShapeDtypeStruct((steps, receivers.shape[1]), jnp.float32),
        ),
        in_specs=[vmem] * 4,
        out_specs=(vmem, vmem),
        scratch_shapes=[
            field,
            field,
            injected,
            pltpu.VMEM((layers * rows, sources.shape[1]), jnp.bfloat16),
            pltpu.VMEM((receivers.shape[1], layers * own), jnp.bfloat16),
        ],
        compiler_params=params,
    )(model, sources, receivers.reshape(-1, 1), values)
    misfit = pl.pallas_call(
        functools.partial(record_kernel, subs),
        out_shape=jax.ShapeDtypeStruct(record.shape, jnp.float32),
        in_specs=[vmem, vmem],
        out_specs=vmem,
        scratch_shapes=[pltpu.VMEM((subs - 1,) + record.shape, jnp.float32)]
        + [pltpu.SemaphoreType.DMA((subs - 1,))] * 2,
        compiler_params=remote_params(1),
    )(record, observed[0])
    values = spread_values(misfit[::-1], receivers[0], width)
    part_gradient = pl.pallas_call(
        functools.partial(backward_kernel, geometry),
        out_shape=jax.ShapeDtypeStruct((layers, own, width), jnp.float32),
        in_specs=[vmem] * 4,
        out_specs=vmem,
        scratch_shapes=[
            field,
            field,
            injected,
            pltpu.VMEM((layers * rows, receivers.shape[1]), jnp.bfloat16),
        ],
        compiler_params=params,
    )(model, receivers, values, laps)

    shots = lax.axis_size("shot")
    if subs == shots and own % (8 * shots) == 0:
        return update_by_strips(part_gradient, model, geometry, subs, shots, remote_params)
    return update_by_slabs(part_gradient, model_field, geometry, subs)


def solution(mesh):
    placed = (
        P(("grp", "sub"), None, None),
        P(("grp", "shot"), None),
        P(("grp", "shot"), None, None),
        P(("grp", "shot"), None),
        P(("grp", "shot"), None, None),
    )
    return jax.shard_map(
        per_device,
        mesh=mesh,
        in_specs=placed,
        out_specs=(P(("grp", "sub"), None, None), P(("grp", "sub"), "shot", None)),
        check_vma=False,
    )
```

```python
import functools

import jax
import jax.numpy as jnp
from jax import lax
from jax.experimental import pallas as pl
from jax.experimental.pallas import tpu as pltpu
from jax.sharding import PartitionSpec as P

ITERS = 6

near_weight = 4.0 / 3.0
far_weight = -1.0 / 12.0
centre_weight = 7.5
step_length = 0.02
tv_bound = 0.01
dual_step = 0.25
primal_step = 0.25
lower_bound = 0.08
upper_bound = 0.22
epsilon = 1e-06

VMEM_LIMIT = 58 * 1024 * 1024


def from_behind(value, axis, steps):
    count = lax.axis_size(axis)
    initial, last = (max(0, -steps), min(count, count - steps))
    return lax.ppermute(value, axis, [(source, source + steps) for source in range(initial, last)])


def forward_part(field, along, upper, last_owner):
    size = field.shape[along]
    first_row = lax.slice_in_dim(field, 0, 1, axis=along)
    remainder = lax.slice_in_dim(field, 1, size, axis=along)
    beyond = jnp.zeros_like(first_row) if upper is None else upper(first_row)
    difference = jnp.concatenate([remainder, beyond], along) - field
    row_index = lax.broadcasted_iota(jnp.int32, field.shape, along)
    return jnp.where(jnp.logical_and(row_index == size - 1, last_owner), 0.0, difference)


def backward_part(dual, along, lower):
    size = dual.shape[along]
    last_row = lax.slice_in_dim(dual, size - 1, size, axis=along)
    before = jnp.zeros_like(last_row) if lower is None else lower(last_row)
    earlier = jnp.concatenate([before, lax.slice_in_dim(dual, 0, size - 1, axis=along)], along)
    return earlier - dual


def project(target, upper_x, lower_x, last_x):
    field = jnp.clip(target, lower_bound, upper_bound)
    extrap = field
    duals = [jnp.zeros_like(field) for along in range(3)]
    for iteration in range(ITERS):
        duals = [
            jnp.clip(
                duals[0] + dual_step * forward_part(extrap, 0, upper_x, last_x), -tv_bound, tv_bound
            ),
            jnp.clip(
                duals[1] + dual_step * forward_part(extrap, 1, None, True), -tv_bound, tv_bound
            ),
            jnp.clip(
                duals[2] + dual_step * forward_part(extrap, 2, None, True), -tv_bound, tv_bound
            ),
        ]
        adjoint = (
            backward_part(duals[0], 0, lower_x)
            + backward_part(duals[1], 1, None)
            + backward_part(duals[2], 2, None)
        )
        following = jnp.clip(
            (field - primal_step * adjoint + primal_step * target) / (1.0 + primal_step),
            lower_bound,
            upper_bound,
        )
        extrap = 2.0 * following - field
        field = following
    return field


def three_pieces(value):
    pieces = []
    for _ in range(2):
        piece = value.astype(jnp.bfloat16)
        pieces.append(piece)
        value = value - piece.astype(jnp.float32)
    return pieces + [value.astype(jnp.bfloat16)]


def one_hot_rows(cells, layers, rows, first_row, height, width):
    lines = cells // width
    layer = lines // height
    row = lines - layer * height - first_row
    inside = jnp.logical_and(row >= 0, row < rows)
    return jnp.where(inside, layer * rows + row, -1)


def advance(model, current, earlier, injected, column, extent, margin, keep, accumulate):
    layers, rows, own, width = extent
    low = (rows - own) // 2 - margin
    count = own + 2 * margin
    span = pl.ds(low, count)
    lane = lax.broadcasted_iota(jnp.int32, (1, width), 1)
    weights = [
        (1, jnp.where(lane >= 1, near_weight, 0.0)),
        (width - 1, jnp.where(lane < width - 1, near_weight, 0.0)),
        (2, jnp.where(lane >= 2, far_weight, 0.0)),
        (width - 2, jnp.where(lane < width - 2, far_weight, 0.0)),
    ]

    def layer_step(layer):
        centre = current[layer + 2, span]
        near = current[layer + 1, span] + current[layer + 3, span]
        far = current[layer, span] + current[layer + 4, span]
        near = near + (pltpu.roll(centre, 1, 0) + pltpu.roll(centre, count - 1, 0))
        far = far + (pltpu.roll(centre, 2, 0) + pltpu.roll(centre, count - 2, 0))
        lap = near_weight * near + far_weight * far - centre_weight * centre
        for shift, weight in weights:
            lap = lap + weight * pltpu.roll(centre, shift, 1)
        start = pl.multiple_of(layer * rows + low, 8)
        following = 2.0 * centre - earlier[layer + 2, span] + model[layer, span] * lap
        following = following + injected[pl.ds(start, count), pl.ds(column, width)]
        earlier[layer + 2, span] = following
        if keep is not None:
            keep(layer, lap[margin : margin + own])
        if accumulate is not None:
            accumulate(layer, following[margin : margin + own])

    block = 4

    def block_step(number, carry):
        for part in range(block):
            layer_step(number * block + part)
        return carry

    lax.fori_loop(0, layers // block, block_step, 0)


def fill_one_hot(target, positions):
    step = 256
    shape = (step, target.shape[1])

    def fill(number, carry):
        begin = pl.multiple_of(number * step, step)
        grid_row = lax.broadcasted_iota(jnp.int32, shape, 0) + begin
        target[pl.ds(begin, step), :] = jnp.where(grid_row == positions, 1.0, 0.0).astype(jnp.bfloat16)
        return carry

    lax.fori_loop(0, target.shape[0] // step, fill, 0)


def inject(spread, values, injected):
    pieces = three_pieces(values)
    blocks = max(1, spread.shape[0] // 896)
    size = spread.shape[0] // blocks

    def block(number, carry):
        span = pl.ds(pl.multiple_of(number * size, 16), size)
        high, middle, low = [
            jnp.dot(spread[span, :], piece, preferred_element_type=jnp.float32) for piece in pieces
        ]
        injected[span, :] = high + (middle + low)
        return carry

    lax.fori_loop(0, blocks, block, 0)


def pair_groups(steps, halo):
    margins = [min(halo, -(-2 * (steps - 1 - 2 * pair) // 8) * 8) for pair in range(steps // 2)]
    groups = []
    for pair, margin in enumerate(margins):
        if pair > 1 and groups[-1][2] == margin:
            groups[-1][1] = pair + 1
        else:
            groups.append([pair, pair + 1, margin])
    return groups


def propagate(
    geometry, subs, shots, model_field, sources, wavelets, receivers, observed,
    wide, model, laps, part, first, second, injected, source_spread, receiver_spread, pick,
    source_table, receiver_table, misfit_table, record, slots,
    send_model, get_model, send_swap, get_swap, send_record, get_record,
):
    layers, rows, own, halo, height, width = geometry
    sub, shot = lax.axis_index("sub"), lax.axis_index("shot")
    slab = layers // subs
    steps = wavelets.shape[0]
    half = slab // 2
    side = lax.rem(shot, 2)
    start_row = sub * own

    wide[:, :halo, :] = jnp.zeros((slab, halo, width), jnp.float32)
    wide[:, halo + height :, :] = jnp.zeros((slab, halo, width), jnp.float32)
    wide[:, halo : halo + height, :] = model_field[...]
    partner = {"sub": sub, "shot": shot + 1 - 2 * side}
    peers = [{"sub": lax.rem(sub + d, subs), "shot": shot} for d in range(1, subs)]

    def rows_of(other):
        return pl.ds(pl.multiple_of(other * own, 8), rows)

    def place(d, which):
        return model.at[pl.ds(lax.rem(sub + subs - d, subs) * slab + which * half, half)]

    sends = []
    for d, peer in enumerate(peers):
        copy = remote(
            wide.at[pl.ds(side * half, half), rows_of(peer["sub"]), :],
            place(0, side), send_model.at[d], get_model.at[d], peer,
        )
        copy.start()
        sends.append(copy)
    for layer in range(slab):
        model[sub * slab + layer] = wide[layer, rows_of(sub), :]

    first[...] = jnp.zeros_like(first)
    second[...] = jnp.zeros_like(second)
    part[...] = jnp.zeros_like(part)
    fill_one_hot(source_spread, one_hot_rows(sources[...], layers, rows, start_row - halo, height, width))

    def lanes_of(cells):
        return (cells - (cells // width) * width).astype(jnp.float32)

    source_table[...] = jnp.zeros_like(source_table)
    source_table[0:steps, :] = wavelets[...]
    source_table[pl.ds(steps, 1), :] = lanes_of(sources[...])
    source_columns = source_table[...].T
    receiver_table[...] = jnp.zeros_like(receiver_table)
    receiver_table[0:1, :] = lanes_of(receivers[...])
    receiver_table[1:2, :] = one_hot_rows(receivers[...], layers, own, start_row, height, width).astype(jnp.float32)
    receiver_columns = receiver_table[...].T
    source_lane = lax.broadcasted_iota(jnp.int32, source_columns.shape, 1)
    source_hot = jnp.where(source_lane.astype(jnp.float32) == source_columns[:, steps : steps + 1], 1.0, 0.0)
    receiver_lane = lax.broadcasted_iota(jnp.int32, receiver_columns.shape, 1)
    receiver_hot = jnp.where(receiver_lane.astype(jnp.float32) == receiver_columns[:, 0:1], 1.0, 0.0)
    cells = layers * own
    owned = receiver_columns[:, 1:2]
    for begin in range(0, cells, 256):
        numbers = lax.broadcasted_iota(jnp.int32, (owned.shape[0], 256), 1) + begin
        pick[:, begin : begin + 256] = jnp.where(numbers.astype(jnp.float32) == owned, 1.0, 0.0).astype(jnp.bfloat16)

    swaps = []
    for d in range(1, subs):
        remote(
            wide.at[pl.ds(side * half, half), rows_of(sub), :],
            place(d, side), send_model.at[d - 1], get_model.at[d - 1], peers[d - 1],
        ).wait_recv()
        copy = remote(place(d, side), place(d, side), send_swap.at[d - 1], get_swap.at[d - 1], partner)
        copy.start()
        swaps.append(copy)
    fill_one_hot(receiver_spread, one_hot_rows(receivers[...], layers, rows, start_row - halo, height, width))

    def column_values(columns, lanes, hot, step):
        return jnp.sum(jnp.where(lanes == step, columns, 0.0), axis=1, keepdims=True) * hot

    def initial(keep_laps):
        def fill(layer, carry):
            first[layer + 2] = injected[pl.ds(pl.multiple_of(layer * rows, 8), rows), pl.ds(0, width)]
            if keep_laps:
                laps[0, layer] = jnp.zeros((own, width), jnp.float32)
            else:
                accumulate(0)(layer, first[layer + 2, halo : halo + own])
            return carry

        lax.fori_loop(0, layers, fill, 0)

    def keep(step):
        def store(layer, lap):
            laps[step, layer] = lap

        return store

    def accumulate(step):
        def add(layer, following):
            part[layer] += following * laps[steps - 1 - step, layer]

        return add

    ones = jnp.ones((8, width), jnp.bfloat16)

    def sample(pair):
        values = [
            three_pieces(field[2 : 2 + layers, halo : halo + own, :].reshape(cells, width))
            for field in (first, second)
        ]
        totals = [jnp.zeros((8, owned.shape[0]), jnp.float32) for _ in range(2)]
        for pieces in zip(*values):
            found = jnp.dot(pick[...], jnp.concatenate(pieces, axis=1), preferred_element_type=jnp.float32)
            for which in range(2):
                piece = (found[:, which * width : (which + 1) * width] * receiver_hot).astype(jnp.bfloat16)
                totals[which] = totals[which] + lax.dot_general(
                    ones, piece, (((1,), (1,)), ((), ())), preferred_element_type=jnp.float32
                )
        for which in range(2):
            record[pl.ds(2 * pair + which, 1), :] = totals[which][0:1]

    extent = (layers, rows, own, width)
    arrived = []

    def run(forward, value_at, spread):
        for begin, end, margin in pair_groups(steps, halo):

            def pair_step(pair, carry):
                inject(spread, jnp.concatenate([value_at(2 * pair), value_at(2 * pair + 1)], axis=1), injected)
                for which, (current, earlier) in enumerate(((second, first), (first, second))):
                    step = 2 * pair + which
                    if begin == 0 and which == 0:
                        initial(forward)
                        if not arrived:
                            for d in range(1, subs):
                                remote(
                                    place(d, 1 - side), place(d, 1 - side),
                                    send_swap.at[d - 1], get_swap.at[d - 1], partner,
                                ).wait_recv()
                            arrived.append(True)
                        continue
                    advance(
                        model, current, earlier, injected, which * width, extent, margin,
                        keep(step) if forward else None, None if forward else accumulate(step),
                    )
                if forward:
                    sample(pair)
                return carry

            if begin == 0:
                pair_step(0, 0)
            else:
                lax.fori_loop(begin, end, pair_step, 0)

    run(True, lambda step: column_values(source_columns, source_lane, source_hot, step), source_spread)
    for copy in sends + swaps:
        copy.wait_send()

    copies = []
    for d, peer in enumerate(peers):
        copy = remote(record, slots.at[d], send_record.at[d], get_record.at[d], peer)
        copy.start()
        copies.append(copy)
    first[...] = jnp.zeros_like(first)
    second[...] = jnp.zeros_like(second)
    misfit_table[...] = jnp.zeros_like(misfit_table)
    total = record[...]
    for d, copy in enumerate(copies):
        copy.wait()
        total = total + slots[d]
    misfit_table[0:steps, :] = total - observed[...]
    misfit_columns = misfit_table[...].T
    run(
        False,
        lambda step: column_values(misfit_columns, receiver_lane, receiver_hot, steps - 1 - step),
        receiver_spread,
    )


def peers_barrier(peers):
    barrier = pltpu.get_barrier_semaphore()
    for peer in peers:
        pl.semaphore_signal(barrier, inc=1, device_id=peer, device_id_type=pl.DeviceIdType.MESH)
    pl.semaphore_wait(barrier, len(peers))


def remote(source, target, send, receive, peer):
    return pltpu.make_async_remote_copy(
        src_ref=source,
        dst_ref=target,
        send_sem=send,
        recv_sem=receive,
        device_id=peer,
        device_id_type=pl.DeviceIdType.MESH,
    )


def update(
    geometry, subs, shots, part, model, updated, gradient,
    near, strip, squares, arrived_squares, above, below,
    field, extrap, target, dual_x, dual_y, dual_z, strip_out, slab_out, brick,
    send_sum, get_sum, send_square, get_square, send_halo, get_halo,
    send_brick, get_brick, send_slab, get_slab, send_on, get_on,
):
    layers, rows, own, halo, height, width = geometry
    slab = layers // subs
    lines = own // shots
    sub, shot = lax.axis_index("sub"), lax.axis_index("shot")

    def at(d_sub, d_shot):
        return {"sub": lax.rem(sub + d_sub, subs), "shot": lax.rem(shot + d_shot, shots)}

    def tiles(first):
        return pl.ds(pl.multiple_of(first, 8), lines)

    group = [(a, b) for a in range(subs) for b in range(shots) if (a, b) != (0, 0)]
    copies = []
    for d in range(1, shots):
        peer = at(0, d)
        copy = remote(
            part.at[:, tiles(peer["shot"] * lines), :], near.at[d - 1], send_sum.at[d - 1], get_sum.at[d - 1], peer
        )
        copy.start()
        copies.append(copy)
    for copy in copies:
        copy.wait()
    square = jnp.zeros((8, width), jnp.float32)
    for layer in range(layers):
        value = part[layer, tiles(shot * lines), :]
        for d in range(shots - 1):
            value = value + near[d, layer]
        strip[layer] = value
        for begin in range(0, lines, 8):
            square = square + value[begin : begin + 8] * value[begin : begin + 8]
    squares[...] = square

    number = sub * shots + shot
    count = subs * shots
    halos = []
    for way, (step, begin, place) in enumerate(((1, lines - 8, above), (count - 1, 0, below))):
        other = lax.rem(number + step, count)
        peer = {"sub": other // shots, "shot": lax.rem(other, shots)}
        copy = remote(
            strip.at[:, pl.ds(begin, 8), :], place, send_halo.at[way], get_halo.at[way], peer
        )
        copy.start()
        halos.append(copy)
    sums = []
    for slot, (a, b) in enumerate(group):
        copy = remote(squares, arrived_squares.at[slot], send_square.at[slot], get_square.at[slot], at(a, b))
        copy.start()
        sums.append(copy)
    here = sub == shot
    bricks = []
    for d in range(subs):
        peer = {"sub": lax.rem(sub + d, subs), "shot": sub}
        bricks.append(
            remote(
                strip.at[pl.ds(peer["sub"] * slab, slab)],
                brick.at[:, tiles(shot * lines), :],
                send_brick.at[d],
                get_brick.at[shot],
                peer,
            )
        )
    for copy in bricks[1:]:
        copy.start()

    @pl.when(jnp.logical_not(here))
    def _():
        bricks[0].start()

    @pl.when(here)
    def _():
        brick[:, tiles(shot * lines), :] = strip[pl.ds(sub * slab, slab)]

    for copy in sums + halos:
        copy.wait()
    total = squares[...]
    for slot in range(len(group)):
        total = total + arrived_squares[slot]
    total = jnp.sum(total, axis=(0, 1), keepdims=True)
    factor = step_length / jnp.sqrt(total / (layers * height * width) + epsilon)
    beside = pl.ds(pl.multiple_of(halo + shot * lines - 8, 8), lines + 16)

    tall = lines + 16
    for layer in range(layers):
        value = jnp.concatenate([above[layer], strip[layer], below[layer]], 0)
        value = model[layer, beside] - factor * value
        target[layer] = value
        value = jnp.clip(value, lower_bound, upper_bound)
        field[layer] = value
        extrap[layer] = value
        for dual in (dual_x, dual_y, dual_z):
            dual[layer] = jnp.zeros((tall, width), jnp.float32)
    grid_row = lax.broadcasted_iota(jnp.int32, (tall, 1), 0) + (number * lines - 8)
    row_weight = jnp.where(jnp.logical_and(grid_row >= 0, grid_row < height - 1), dual_step, 0.0)
    lane = lax.broadcasted_iota(jnp.int32, (1, width), 1)
    lane_weight = jnp.where(lane < width - 1, dual_step, 0.0)

    def iteration(turn, carry):
        before = jnp.zeros((tall, width), jnp.float32)
        for layer in range(layers):
            value = extrap[layer]
            along_x = before
            if layer < layers - 1:
                along_x = dual_x[layer] + dual_step * (extrap[layer + 1] - value)
                along_x = jnp.clip(along_x, -tv_bound, tv_bound)
                dual_x[layer] = along_x
            else:
                along_x = jnp.zeros_like(before)
            along_y = dual_y[layer] + row_weight * (pltpu.roll(value, tall - 1, 0) - value)
            along_y = jnp.clip(along_y, -tv_bound, tv_bound)
            dual_y[layer] = along_y
            along_z = dual_z[layer] + lane_weight * (pltpu.roll(value, width - 1, 1) - value)
            along_z = jnp.clip(along_z, -tv_bound, tv_bound)
            dual_z[layer] = along_z
            adjoint = (
                (before - along_x)
                + (pltpu.roll(along_y, 1, 0) - along_y)
                + (pltpu.roll(along_z, 1, 1) - along_z)
            )
            old = field[layer]
            new = (old - primal_step * adjoint + primal_step * target[layer]) * (1.0 / (1.0 + primal_step))
            new = jnp.clip(new, lower_bound, upper_bound)
            extrap[layer] = 2.0 * new - old
            field[layer] = new
            before = along_x
        return carry

    lax.fori_loop(0, ITERS, iteration, 0)
    for layer in range(layers):
        strip_out[layer] = field[layer, 8 : 8 + lines]

    def place(d_sub, d_shot):
        origin_sub = lax.rem(sub + subs - d_sub, subs)
        origin_shot = lax.rem(shot + shots - d_shot, shots)
        return slab_out.at[:, tiles(origin_sub * own + origin_shot * lines), :]

    slabs = []
    for d in range(1, subs):
        peer = at(d, 0)
        copy = remote(
            strip_out.at[pl.ds(peer["sub"] * slab, slab)], place(0, 0), send_slab.at[d - 1], get_slab.at[d - 1], peer
        )
        copy.start()
        slabs.append(copy)
    slab_out[:, tiles(sub * own + shot * lines), :] = strip_out[pl.ds(sub * slab, slab)]
    onward = []
    for d in range(subs):
        if d > 0:
            remote(
                strip_out.at[pl.ds(sub * slab, slab)], place(d, 0), send_slab.at[d - 1], get_slab.at[d - 1], at(d, 0)
            ).wait_recv()
        for e in range(1, shots):
            copy = remote(place(d, 0), place(d, 0), send_on.at[d, e - 1], get_on.at[d, e - 1], at(0, e))
            copy.start()
            onward.append((d, e, copy))
    for copy in bricks[1:]:
        copy.wait_send()

    @pl.when(jnp.logical_not(here))
    def _():
        bricks[0].wait_send()

    for origin in range(shots):

        @pl.when(jnp.logical_not(jnp.logical_and(here, shot == origin)))
        def _():
            remote(
                strip.at[pl.ds(0, slab)],
                brick.at[:, pl.ds(origin * lines, lines), :],
                send_brick.at[0],
                get_brick.at[origin],
                at(1, 0),
            ).wait_recv()

    gradient[...] = brick[...]
    for copy in slabs:
        copy.wait_send()
    for d, e, copy in onward:
        copy.wait_send()
        remote(place(d, e), place(d, e), send_on.at[d, e - 1], get_on.at[d, e - 1], at(0, e)).wait_recv()
    updated[...] = slab_out[...]


PROPAGATE_SCRATCH = 21


def step_kernel(geometry, subs, shots, strips, *refs):
    inputs, refs = refs[:5], refs[5:]
    if strips:
        updated, gradient = refs[:2]
        scratch = refs[2:]
        laps_on = scratch[:3]
        part, scratch = scratch[3], scratch[4:]
    else:
        part, laps_on, scratch = refs[0], refs[1:4], refs[4:]
    wide, model, laps = laps_on
    own_scratch, rest = scratch[: PROPAGATE_SCRATCH - 4], scratch[PROPAGATE_SCRATCH - 4 :]
    sub, shot = lax.axis_index("sub"), lax.axis_index("shot")
    if strips:
        group = [(a, b) for a in range(subs) for b in range(shots) if (a, b) != (0, 0)]
        peers_barrier(
            [{"sub": lax.rem(sub + a, subs), "shot": lax.rem(shot + b, shots)} for a, b in group]
        )
    else:
        peers_barrier(
            [{"sub": lax.rem(sub + a, subs), "shot": shot} for a in range(1, subs)]
            + [{"sub": sub, "shot": shot + 1 - 2 * lax.rem(shot, 2)}]
        )
    propagate(geometry, subs, shots, *inputs, wide, model, laps, part, *own_scratch)
    if strips:
        update(geometry, subs, shots, part, model, updated, gradient, *rest)


def update_by_slabs(part, model_field, geometry, subs):
    layers, rows, own, halo, height, width = geometry
    slab = layers // subs
    local_gradient = lax.all_to_all(part.reshape(subs, slab, own, width), "sub", 0, 0)
    local_gradient = jnp.swapaxes(local_gradient, 0, 1).reshape(slab, height, width)
    last_x = lax.axis_index("sub") == subs - 1
    slab_gradient = lax.psum(local_gradient, "shot")
    square_sum = lax.psum(jnp.sum(slab_gradient * slab_gradient), "sub")
    grad_scale = jnp.sqrt(square_sum / (layers * height * width) + epsilon)
    target = model_field - step_length * (slab_gradient / grad_scale)

    def slab_upper(layer):
        return from_behind(layer, "sub", -1)

    def slab_lower(layer):
        return from_behind(layer, "sub", 1)

    updated_model = project(target, slab_upper, slab_lower, last_x)
    brick_rows = height // lax.axis_size("shot")
    gradient = lax.dynamic_slice_in_dim(
        slab_gradient, lax.axis_index("shot") * brick_rows, brick_rows, 1
    )
    return (updated_model, gradient)


def per_device(model_field, source_index, wavelets, receiver_index, observed):
    slab, height, width = model_field.shape
    subs, shots = lax.axis_size("sub"), lax.axis_size("shot")
    layers = slab * subs
    own = height // subs
    steps = wavelets.shape[1]
    halo = 2 * steps
    rows = own + 2 * halo
    geometry = (layers, rows, own, halo, height, width)
    points, receivers = source_index.shape[1], receiver_index.shape[1]
    strips = subs == shots and own % (8 * shots) == 0
    lines = own // shots
    tall = lines + 16
    others = subs * shots - 1
    vmem = pl.BlockSpec(memory_space=pltpu.VMEM)

    def space(*shape, dtype=jnp.float32):
        return pltpu.VMEM(shape, dtype)

    def sems(*shape):
        return pltpu.SemaphoreType.DMA(shape)

    scratch = [space(slab, height + 2 * halo, width), space(layers, rows, width), space(steps, layers, own, width)]
    if strips:
        scratch.append(space(layers, own, width))
    scratch += [
        space(layers + 4, rows, width),
        space(layers + 4, rows, width),
        space(layers * rows, 2 * width),
        space(layers * rows, points, dtype=jnp.bfloat16),
        space(layers * rows, receivers, dtype=jnp.bfloat16),
        space(receivers, layers * own, dtype=jnp.bfloat16),
        space(width, points),
        space(width, receivers),
        space(width, receivers),
        space(steps, receivers),
        space(subs - 1, steps, receivers),
    ] + [sems(subs - 1)] * 6
    if strips:
        scratch += [
            space(shots - 1, layers, lines, width),
            space(layers, lines, width),
            space(8, width),
            space(others, 8, width),
            space(layers, 8, width),
            space(layers, 8, width),
        ]
        scratch += [space(layers, tall, width)] * 6
        scratch += [space(layers, lines, width), space(slab, height, width), space(slab, own, width)]
        scratch += [sems(shots - 1)] * 2 + [sems(others)] * 2 + [sems(2)] * 2 + [sems(subs), sems(shots)]
        scratch += [sems(subs - 1)] * 2 + [sems(subs, shots - 1)] * 2
        out_shape = (
            jax.ShapeDtypeStruct((slab, height, width), jnp.float32),
            jax.ShapeDtypeStruct((slab, own, width), jnp.float32),
        )
        out_specs = (vmem, vmem)
    else:
        out_shape = jax.ShapeDtypeStruct((layers, own, width), jnp.float32)
        out_specs = vmem
    result = pl.pallas_call(
        functools.partial(step_kernel, geometry, subs, shots, strips),
        out_shape=out_shape,
        in_specs=[vmem] * 5,
        out_specs=out_specs,
        scratch_shapes=scratch,
        compiler_params=pltpu.CompilerParams(
            collective_id=0, has_side_effects=True, vmem_limit_bytes=VMEM_LIMIT
        ),
    )(model_field, source_index, wavelets[0], receiver_index, observed[0])
    if strips:
        return result
    return update_by_slabs(result, model_field, geometry, subs)


def solution(mesh):
    placed = (
        P(("grp", "sub"), None, None),
        P(("grp", "shot"), None),
        P(("grp", "shot"), None, None),
        P(("grp", "shot"), None),
        P(("grp", "shot"), None, None),
    )
    return jax.shard_map(
        per_device,
        mesh=mesh,
        in_specs=placed,
        out_specs=(P(("grp", "sub"), None, None), P(("grp", "sub"), "shot", None)),
        check_vma=False,
    )
```

```python
import functools

import jax
import jax.numpy as jnp
from jax import lax
from jax.experimental import pallas as pl
from jax.experimental.pallas import tpu as pltpu
from jax.sharding import PartitionSpec as P

ITERS = 6

near_weight = 4.0 / 3.0
far_weight = -1.0 / 12.0
centre_weight = 7.5
step_length = 0.02
tv_bound = 0.01
dual_step = 0.25
primal_step = 0.25
lower_bound = 0.08
upper_bound = 0.22
epsilon = 1e-06

VMEM_LIMIT = 58 * 1024 * 1024


def from_behind(value, axis, steps):
    count = lax.axis_size(axis)
    initial, last = (max(0, -steps), min(count, count - steps))
    return lax.ppermute(value, axis, [(source, source + steps) for source in range(initial, last)])


def forward_part(field, along, upper, last_owner):
    size = field.shape[along]
    first_row = lax.slice_in_dim(field, 0, 1, axis=along)
    remainder = lax.slice_in_dim(field, 1, size, axis=along)
    beyond = jnp.zeros_like(first_row) if upper is None else upper(first_row)
    difference = jnp.concatenate([remainder, beyond], along) - field
    row_index = lax.broadcasted_iota(jnp.int32, field.shape, along)
    return jnp.where(jnp.logical_and(row_index == size - 1, last_owner), 0.0, difference)


def backward_part(dual, along, lower):
    size = dual.shape[along]
    last_row = lax.slice_in_dim(dual, size - 1, size, axis=along)
    before = jnp.zeros_like(last_row) if lower is None else lower(last_row)
    earlier = jnp.concatenate([before, lax.slice_in_dim(dual, 0, size - 1, axis=along)], along)
    return earlier - dual


def project(target, upper_x, lower_x, last_x):
    field = jnp.clip(target, lower_bound, upper_bound)
    extrap = field
    duals = [jnp.zeros_like(field) for along in range(3)]
    for iteration in range(ITERS):
        duals = [
            jnp.clip(
                duals[0] + dual_step * forward_part(extrap, 0, upper_x, last_x), -tv_bound, tv_bound
            ),
            jnp.clip(
                duals[1] + dual_step * forward_part(extrap, 1, None, True), -tv_bound, tv_bound
            ),
            jnp.clip(
                duals[2] + dual_step * forward_part(extrap, 2, None, True), -tv_bound, tv_bound
            ),
        ]
        adjoint = (
            backward_part(duals[0], 0, lower_x)
            + backward_part(duals[1], 1, None)
            + backward_part(duals[2], 2, None)
        )
        following = jnp.clip(
            (field - primal_step * adjoint + primal_step * target) / (1.0 + primal_step),
            lower_bound,
            upper_bound,
        )
        extrap = 2.0 * following - field
        field = following
    return field


def three_pieces(value):
    pieces = []
    for _ in range(2):
        piece = value.astype(jnp.bfloat16)
        pieces.append(piece)
        value = value - piece.astype(jnp.float32)
    return pieces + [value.astype(jnp.bfloat16)]


def one_hot_rows(cells, layers, rows, first_row, height, width):
    lines = cells // width
    layer = lines // height
    row = lines - layer * height - first_row
    inside = jnp.logical_and(row >= 0, row < rows)
    return jnp.where(inside, layer * rows + row, -1)


def advance(model, current, earlier, injected, column, extent, margin, keep, accumulate):
    layers, rows, own, width = extent
    low = (rows - own) // 2 - margin
    count = own + 2 * margin
    span = pl.ds(low, count)
    lane = lax.broadcasted_iota(jnp.int32, (1, width), 1)
    weights = [
        (1, jnp.where(lane >= 1, near_weight, 0.0)),
        (width - 1, jnp.where(lane < width - 1, near_weight, 0.0)),
        (2, jnp.where(lane >= 2, far_weight, 0.0)),
        (width - 2, jnp.where(lane < width - 2, far_weight, 0.0)),
    ]

    def layer_step(layer):
        centre = current[layer + 2, span]
        near = current[layer + 1, span] + current[layer + 3, span]
        far = current[layer, span] + current[layer + 4, span]
        near = near + (pltpu.roll(centre, 1, 0) + pltpu.roll(centre, count - 1, 0))
        far = far + (pltpu.roll(centre, 2, 0) + pltpu.roll(centre, count - 2, 0))
        lap = near_weight * near + far_weight * far - centre_weight * centre
        for shift, weight in weights:
            lap = lap + weight * pltpu.roll(centre, shift, 1)
        start = pl.multiple_of(layer * rows + low, 8)
        following = 2.0 * centre - earlier[layer + 2, span] + model[layer, span] * lap
        following = following + injected[pl.ds(start, count), pl.ds(column, width)]
        earlier[layer + 2, span] = following
        if keep is not None:
            keep(layer, lap[margin : margin + own])
        if accumulate is not None:
            accumulate(layer, following[margin : margin + own])

    block = 8

    def block_step(number, carry):
        for part in range(block):
            layer_step(number * block + part)
        return carry

    lax.fori_loop(0, layers // block, block_step, 0)


def fill_one_hot(target, positions):
    step = 256
    shape = (step, target.shape[1])

    def fill(number, carry):
        begin = pl.multiple_of(number * step, step)
        grid_row = lax.broadcasted_iota(jnp.int32, shape, 0) + begin
        target[pl.ds(begin, step), :] = jnp.where(grid_row == positions, 1.0, 0.0).astype(jnp.bfloat16)
        return carry

    lax.fori_loop(0, target.shape[0] // step, fill, 0)


def inject(spread, values, injected):
    pieces = three_pieces(values)
    blocks = max(1, spread.shape[0] // 896)
    size = spread.shape[0] // blocks

    def block(number, carry):
        span = pl.ds(pl.multiple_of(number * size, 16), size)
        high, middle, low = [
            jnp.dot(spread[span, :], piece, preferred_element_type=jnp.float32) for piece in pieces
        ]
        injected[span, :] = high + (middle + low)
        return carry

    lax.fori_loop(0, blocks, block, 0)


def pair_groups(steps, halo):
    margins = [min(halo, -(-2 * (steps - 1 - 2 * pair) // 8) * 8) for pair in range(steps // 2)]
    groups = []
    for pair, margin in enumerate(margins):
        if pair > 1 and groups[-1][2] == margin:
            groups[-1][1] = pair + 1
        else:
            groups.append([pair, pair + 1, margin])
    return groups


def propagate(
    geometry, subs, shots, model_field, sources, wavelets, receivers, observed,
    wide, model, laps, part, first, second, injected, source_spread, receiver_spread, pick,
    source_table, receiver_table, misfit_table, record, slots,
    send_model, get_model, send_swap, get_swap, send_record, get_record,
):
    layers, rows, own, halo, height, width = geometry
    sub, shot = lax.axis_index("sub"), lax.axis_index("shot")
    slab = layers // subs
    steps = wavelets.shape[0]
    half = slab // 2
    side = lax.rem(shot, 2)
    start_row = sub * own

    wide[:, :halo, :] = jnp.zeros((slab, halo, width), jnp.float32)
    wide[:, halo + height :, :] = jnp.zeros((slab, halo, width), jnp.float32)
    wide[:, halo : halo + height, :] = model_field[...]
    partner = {"sub": sub, "shot": shot + 1 - 2 * side}
    peers = [{"sub": lax.rem(sub + d, subs), "shot": shot} for d in range(1, subs)]

    def rows_of(other):
        return pl.ds(pl.multiple_of(other * own, 8), rows)

    def place(d, which):
        return model.at[pl.ds(lax.rem(sub + subs - d, subs) * slab + which * half, half)]

    sends = []
    for d, peer in enumerate(peers):
        copy = remote(
            wide.at[pl.ds(side * half, half), rows_of(peer["sub"]), :],
            place(0, side), send_model.at[d], get_model.at[d], peer,
        )
        copy.start()
        sends.append(copy)
    for layer in range(slab):
        model[sub * slab + layer] = wide[layer, rows_of(sub), :]

    first[...] = jnp.zeros_like(first)
    second[...] = jnp.zeros_like(second)
    part[...] = jnp.zeros_like(part)
    fill_one_hot(source_spread, one_hot_rows(sources[...], layers, rows, start_row - halo, height, width))

    def lanes_of(cells):
        return (cells - (cells // width) * width).astype(jnp.float32)

    source_table[...] = jnp.zeros_like(source_table)
    source_table[0:steps, :] = wavelets[...]
    source_table[pl.ds(steps, 1), :] = lanes_of(sources[...])
    source_columns = source_table[...].T
    receiver_table[...] = jnp.zeros_like(receiver_table)
    receiver_table[0:1, :] = lanes_of(receivers[...])
    receiver_table[1:2, :] = one_hot_rows(receivers[...], layers, own, start_row, height, width).astype(jnp.float32)
    receiver_columns = receiver_table[...].T
    source_lane = lax.broadcasted_iota(jnp.int32, source_columns.shape, 1)
    source_hot = jnp.where(source_lane.astype(jnp.float32) == source_columns[:, steps : steps + 1], 1.0, 0.0)
    receiver_lane = lax.broadcasted_iota(jnp.int32, receiver_columns.shape, 1)
    receiver_hot = jnp.where(receiver_lane.astype(jnp.float32) == receiver_columns[:, 0:1], 1.0, 0.0)
    cells = layers * own
    owned = receiver_columns[:, 1:2]
    for begin in range(0, cells, 256):
        numbers = lax.broadcasted_iota(jnp.int32, (owned.shape[0], 256), 1) + begin
        pick[:, begin : begin + 256] = jnp.where(numbers.astype(jnp.float32) == owned, 1.0, 0.0).astype(jnp.bfloat16)

    swaps = []
    for d in range(1, subs):
        remote(
            wide.at[pl.ds(side * half, half), rows_of(sub), :],
            place(d, side), send_model.at[d - 1], get_model.at[d - 1], peers[d - 1],
        ).wait_recv()
        copy = remote(place(d, side), place(d, side), send_swap.at[d - 1], get_swap.at[d - 1], partner)
        copy.start()
        swaps.append(copy)
    fill_one_hot(receiver_spread, one_hot_rows(receivers[...], layers, rows, start_row - halo, height, width))

    def column_values(columns, lanes, hot, step):
        return jnp.sum(jnp.where(lanes == step, columns, 0.0), axis=1, keepdims=True) * hot

    def initial(keep_laps):
        def fill(layer, carry):
            first[layer + 2] = injected[pl.ds(pl.multiple_of(layer * rows, 8), rows), pl.ds(0, width)]
            if keep_laps:
                laps[0, layer] = jnp.zeros((own, width), jnp.float32)
            else:
                accumulate(0)(layer, first[layer + 2, halo : halo + own])
            return carry

        lax.fori_loop(0, layers, fill, 0)

    def keep(step):
        def store(layer, lap):
            laps[step, layer] = lap

        return store

    def accumulate(step):
        def add(layer, following):
            part[layer] += following * laps[steps - 1 - step, layer]

        return add

    ones = jnp.ones((8, width), jnp.bfloat16)

    def sample(pair):
        values = [
            three_pieces(field[2 : 2 + layers, halo : halo + own, :].reshape(cells, width))
            for field in (first, second)
        ]
        totals = [jnp.zeros((8, owned.shape[0]), jnp.float32) for _ in range(2)]
        for pieces in zip(*values):
            found = jnp.dot(pick[...], jnp.concatenate(pieces, axis=1), preferred_element_type=jnp.float32)
            for which in range(2):
                piece = (found[:, which * width : (which + 1) * width] * receiver_hot).astype(jnp.bfloat16)
                totals[which] = totals[which] + lax.dot_general(
                    ones, piece, (((1,), (1,)), ((), ())), preferred_element_type=jnp.float32
                )
        for which in range(2):
            record[pl.ds(2 * pair + which, 1), :] = totals[which][0:1]

    extent = (layers, rows, own, width)
    arrived = []

    def run(forward, value_at, spread):
        for begin, end, margin in pair_groups(steps, halo):

            def pair_step(pair, carry):
                inject(spread, jnp.concatenate([value_at(2 * pair), value_at(2 * pair + 1)], axis=1), injected)
                for which, (current, earlier) in enumerate(((second, first), (first, second))):
                    step = 2 * pair + which
                    if begin == 0 and which == 0:
                        initial(forward)
                        if not arrived:
                            for d in range(1, subs):
                                remote(
                                    place(d, 1 - side), place(d, 1 - side),
                                    send_swap.at[d - 1], get_swap.at[d - 1], partner,
                                ).wait_recv()
                            arrived.append(True)
                        continue
                    advance(
                        model, current, earlier, injected, which * width, extent, margin,
                        keep(step) if forward else None, None if forward else accumulate(step),
                    )
                if forward:
                    sample(pair)
                return carry

            if begin == 0:
                pair_step(0, 0)
            else:
                lax.fori_loop(begin, end, pair_step, 0)

    run(True, lambda step: column_values(source_columns, source_lane, source_hot, step), source_spread)
    for copy in sends + swaps:
        copy.wait_send()

    copies = []
    for d, peer in enumerate(peers):
        copy = remote(record, slots.at[d], send_record.at[d], get_record.at[d], peer)
        copy.start()
        copies.append(copy)
    first[...] = jnp.zeros_like(first)
    second[...] = jnp.zeros_like(second)
    misfit_table[...] = jnp.zeros_like(misfit_table)
    total = record[...]
    for d, copy in enumerate(copies):
        copy.wait()
        total = total + slots[d]
    misfit_table[0:steps, :] = total - observed[...]
    misfit_columns = misfit_table[...].T
    run(
        False,
        lambda step: column_values(misfit_columns, receiver_lane, receiver_hot, steps - 1 - step),
        receiver_spread,
    )


def peers_barrier(peers):
    barrier = pltpu.get_barrier_semaphore()
    for peer in peers:
        pl.semaphore_signal(barrier, inc=1, device_id=peer, device_id_type=pl.DeviceIdType.MESH)
    pl.semaphore_wait(barrier, len(peers))


def remote(source, target, send, receive, peer):
    return pltpu.make_async_remote_copy(
        src_ref=source,
        dst_ref=target,
        send_sem=send,
        recv_sem=receive,
        device_id=peer,
        device_id_type=pl.DeviceIdType.MESH,
    )


def update(
    geometry, subs, shots, part, model, updated, gradient,
    near, strip, squares, arrived_squares, above, below,
    field, extrap, target, dual_x, dual_y, dual_z, strip_out, slab_out, brick,
    send_sum, get_sum, send_square, get_square, send_halo, get_halo,
    send_brick, get_brick, send_slab, get_slab, send_on, get_on,
):
    layers, rows, own, halo, height, width = geometry
    slab = layers // subs
    lines = own // shots
    sub, shot = lax.axis_index("sub"), lax.axis_index("shot")

    def at(d_sub, d_shot):
        return {"sub": lax.rem(sub + d_sub, subs), "shot": lax.rem(shot + d_shot, shots)}

    def tiles(first):
        return pl.ds(pl.multiple_of(first, 8), lines)

    group = [(a, b) for a in range(subs) for b in range(shots) if (a, b) != (0, 0)]
    copies = []
    for d in range(1, shots):
        peer = at(0, d)
        copy = remote(
            part.at[:, tiles(peer["shot"] * lines), :], near.at[d - 1], send_sum.at[d - 1], get_sum.at[d - 1], peer
        )
        copy.start()
        copies.append(copy)
    for copy in copies:
        copy.wait()
    square = jnp.zeros((8, width), jnp.float32)
    for layer in range(layers):
        value = part[layer, tiles(shot * lines), :]
        for d in range(shots - 1):
            value = value + near[d, layer]
        strip[layer] = value
        for begin in range(0, lines, 8):
            square = square + value[begin : begin + 8] * value[begin : begin + 8]
    squares[...] = square

    number = sub * shots + shot
    count = subs * shots
    halos = []
    for way, (step, begin, place) in enumerate(((1, lines - 8, above), (count - 1, 0, below))):
        other = lax.rem(number + step, count)
        peer = {"sub": other // shots, "shot": lax.rem(other, shots)}
        copy = remote(
            strip.at[:, pl.ds(begin, 8), :], place, send_halo.at[way], get_halo.at[way], peer
        )
        copy.start()
        halos.append(copy)
    sums = []
    for slot, (a, b) in enumerate(group):
        copy = remote(squares, arrived_squares.at[slot], send_square.at[slot], get_square.at[slot], at(a, b))
        copy.start()
        sums.append(copy)
    here = sub == shot
    bricks = []
    for d in range(subs):
        peer = {"sub": lax.rem(sub + d, subs), "shot": sub}
        bricks.append(
            remote(
                strip.at[pl.ds(peer["sub"] * slab, slab)],
                brick.at[:, tiles(shot * lines), :],
                send_brick.at[d],
                get_brick.at[shot],
                peer,
            )
        )
    for copy in bricks[1:]:
        copy.start()

    @pl.when(jnp.logical_not(here))
    def _():
        bricks[0].start()

    @pl.when(here)
    def _():
        brick[:, tiles(shot * lines), :] = strip[pl.ds(sub * slab, slab)]

    for copy in sums + halos:
        copy.wait()
    total = squares[...]
    for slot in range(len(group)):
        total = total + arrived_squares[slot]
    total = jnp.sum(total, axis=(0, 1), keepdims=True)
    factor = step_length / jnp.sqrt(total / (layers * height * width) + epsilon)
    beside = pl.ds(pl.multiple_of(halo + shot * lines - 8, 8), lines + 16)

    tall = lines + 16
    for layer in range(layers):
        value = jnp.concatenate([above[layer], strip[layer], below[layer]], 0)
        value = model[layer, beside] - factor * value
        target[layer] = value
        value = jnp.clip(value, lower_bound, upper_bound)
        field[layer] = value
        extrap[layer] = value
        for dual in (dual_x, dual_y, dual_z):
            dual[layer] = jnp.zeros((tall, width), jnp.float32)
    grid_row = lax.broadcasted_iota(jnp.int32, (tall, 1), 0) + (number * lines - 8)
    row_weight = jnp.where(jnp.logical_and(grid_row >= 0, grid_row < height - 1), dual_step, 0.0)
    lane = lax.broadcasted_iota(jnp.int32, (1, width), 1)
    lane_weight = jnp.where(lane < width - 1, dual_step, 0.0)

    def iteration(turn, carry):
        before = jnp.zeros((tall, width), jnp.float32)
        for layer in range(layers):
            value = extrap[layer]
            along_x = before
            if layer < layers - 1:
                along_x = dual_x[layer] + dual_step * (extrap[layer + 1] - value)
                along_x = jnp.clip(along_x, -tv_bound, tv_bound)
                dual_x[layer] = along_x
            else:
                along_x = jnp.zeros_like(before)
            along_y = dual_y[layer] + row_weight * (pltpu.roll(value, tall - 1, 0) - value)
            along_y = jnp.clip(along_y, -tv_bound, tv_bound)
            dual_y[layer] = along_y
            along_z = dual_z[layer] + lane_weight * (pltpu.roll(value, width - 1, 1) - value)
            along_z = jnp.clip(along_z, -tv_bound, tv_bound)
            dual_z[layer] = along_z
            adjoint = (
                (before - along_x)
                + (pltpu.roll(along_y, 1, 0) - along_y)
                + (pltpu.roll(along_z, 1, 1) - along_z)
            )
            old = field[layer]
            new = (old - primal_step * adjoint + primal_step * target[layer]) * (1.0 / (1.0 + primal_step))
            new = jnp.clip(new, lower_bound, upper_bound)
            extrap[layer] = 2.0 * new - old
            field[layer] = new
            before = along_x
        return carry

    lax.fori_loop(0, ITERS, iteration, 0)
    for layer in range(layers):
        strip_out[layer] = field[layer, 8 : 8 + lines]

    def place(d_sub, d_shot):
        origin_sub = lax.rem(sub + subs - d_sub, subs)
        origin_shot = lax.rem(shot + shots - d_shot, shots)
        return slab_out.at[:, tiles(origin_sub * own + origin_shot * lines), :]

    slabs = []
    for d in range(1, subs):
        peer = at(d, 0)
        copy = remote(
            strip_out.at[pl.ds(peer["sub"] * slab, slab)], place(0, 0), send_slab.at[d - 1], get_slab.at[d - 1], peer
        )
        copy.start()
        slabs.append(copy)
    slab_out[:, tiles(sub * own + shot * lines), :] = strip_out[pl.ds(sub * slab, slab)]
    onward = []
    for d in range(subs):
        if d > 0:
            remote(
                strip_out.at[pl.ds(sub * slab, slab)], place(d, 0), send_slab.at[d - 1], get_slab.at[d - 1], at(d, 0)
            ).wait_recv()
        for e in range(1, shots):
            copy = remote(place(d, 0), place(d, 0), send_on.at[d, e - 1], get_on.at[d, e - 1], at(0, e))
            copy.start()
            onward.append((d, e, copy))
    for copy in bricks[1:]:
        copy.wait_send()

    @pl.when(jnp.logical_not(here))
    def _():
        bricks[0].wait_send()

    for origin in range(shots):

        @pl.when(jnp.logical_not(jnp.logical_and(here, shot == origin)))
        def _():
            remote(
                strip.at[pl.ds(0, slab)],
                brick.at[:, pl.ds(origin * lines, lines), :],
                send_brick.at[0],
                get_brick.at[origin],
                at(1, 0),
            ).wait_recv()

    gradient[...] = brick[...]
    for copy in slabs:
        copy.wait_send()
    for d, e, copy in onward:
        copy.wait_send()
        remote(place(d, e), place(d, e), send_on.at[d, e - 1], get_on.at[d, e - 1], at(0, e)).wait_recv()
    updated[...] = slab_out[...]


PROPAGATE_SCRATCH = 21


def step_kernel(geometry, subs, shots, strips, *refs):
    inputs, refs = refs[:5], refs[5:]
    if strips:
        updated, gradient = refs[:2]
        scratch = refs[2:]
        laps_on = scratch[:3]
        part, scratch = scratch[3], scratch[4:]
    else:
        part, laps_on, scratch = refs[0], refs[1:4], refs[4:]
    wide, model, laps = laps_on
    own_scratch, rest = scratch[: PROPAGATE_SCRATCH - 4], scratch[PROPAGATE_SCRATCH - 4 :]
    sub, shot = lax.axis_index("sub"), lax.axis_index("shot")
    if strips:
        group = [(a, b) for a in range(subs) for b in range(shots) if (a, b) != (0, 0)]
        peers_barrier(
            [{"sub": lax.rem(sub + a, subs), "shot": lax.rem(shot + b, shots)} for a, b in group]
        )
    else:
        peers_barrier(
            [{"sub": lax.rem(sub + a, subs), "shot": shot} for a in range(1, subs)]
            + [{"sub": sub, "shot": shot + 1 - 2 * lax.rem(shot, 2)}]
        )
    propagate(geometry, subs, shots, *inputs, wide, model, laps, part, *own_scratch)
    if strips:
        update(geometry, subs, shots, part, model, updated, gradient, *rest)


def update_by_slabs(part, model_field, geometry, subs):
    layers, rows, own, halo, height, width = geometry
    slab = layers // subs
    local_gradient = lax.all_to_all(part.reshape(subs, slab, own, width), "sub", 0, 0)
    local_gradient = jnp.swapaxes(local_gradient, 0, 1).reshape(slab, height, width)
    last_x = lax.axis_index("sub") == subs - 1
    slab_gradient = lax.psum(local_gradient, "shot")
    square_sum = lax.psum(jnp.sum(slab_gradient * slab_gradient), "sub")
    grad_scale = jnp.sqrt(square_sum / (layers * height * width) + epsilon)
    target = model_field - step_length * (slab_gradient / grad_scale)

    def slab_upper(layer):
        return from_behind(layer, "sub", -1)

    def slab_lower(layer):
        return from_behind(layer, "sub", 1)

    updated_model = project(target, slab_upper, slab_lower, last_x)
    brick_rows = height // lax.axis_size("shot")
    gradient = lax.dynamic_slice_in_dim(
        slab_gradient, lax.axis_index("shot") * brick_rows, brick_rows, 1
    )
    return (updated_model, gradient)


def per_device(model_field, source_index, wavelets, receiver_index, observed):
    slab, height, width = model_field.shape
    subs, shots = lax.axis_size("sub"), lax.axis_size("shot")
    layers = slab * subs
    own = height // subs
    steps = wavelets.shape[1]
    halo = 2 * steps
    rows = own + 2 * halo
    geometry = (layers, rows, own, halo, height, width)
    points, receivers = source_index.shape[1], receiver_index.shape[1]
    strips = subs == shots and own % (8 * shots) == 0
    lines = own // shots
    tall = lines + 16
    others = subs * shots - 1
    vmem = pl.BlockSpec(memory_space=pltpu.VMEM)

    def space(*shape, dtype=jnp.float32):
        return pltpu.VMEM(shape, dtype)

    def sems(*shape):
        return pltpu.SemaphoreType.DMA(shape)

    scratch = [space(slab, height + 2 * halo, width), space(layers, rows, width), space(steps, layers, own, width)]
    if strips:
        scratch.append(space(layers, own, width))
    scratch += [
        space(layers + 4, rows, width),
        space(layers + 4, rows, width),
        space(layers * rows, 2 * width),
        space(layers * rows, points, dtype=jnp.bfloat16),
        space(layers * rows, receivers, dtype=jnp.bfloat16),
        space(receivers, layers * own, dtype=jnp.bfloat16),
        space(width, points),
        space(width, receivers),
        space(width, receivers),
        space(steps, receivers),
        space(subs - 1, steps, receivers),
    ] + [sems(subs - 1)] * 6
    if strips:
        scratch += [
            space(shots - 1, layers, lines, width),
            space(layers, lines, width),
            space(8, width),
            space(others, 8, width),
            space(layers, 8, width),
            space(layers, 8, width),
        ]
        scratch += [space(layers, tall, width)] * 6
        scratch += [space(layers, lines, width), space(slab, height, width), space(slab, own, width)]
        scratch += [sems(shots - 1)] * 2 + [sems(others)] * 2 + [sems(2)] * 2 + [sems(subs), sems(shots)]
        scratch += [sems(subs - 1)] * 2 + [sems(subs, shots - 1)] * 2
        out_shape = (
            jax.ShapeDtypeStruct((slab, height, width), jnp.float32),
            jax.ShapeDtypeStruct((slab, own, width), jnp.float32),
        )
        out_specs = (vmem, vmem)
    else:
        out_shape = jax.ShapeDtypeStruct((layers, own, width), jnp.float32)
        out_specs = vmem
    result = pl.pallas_call(
        functools.partial(step_kernel, geometry, subs, shots, strips),
        out_shape=out_shape,
        in_specs=[vmem] * 5,
        out_specs=out_specs,
        scratch_shapes=scratch,
        compiler_params=pltpu.CompilerParams(
            collective_id=0, has_side_effects=True, vmem_limit_bytes=VMEM_LIMIT
        ),
    )(model_field, source_index, wavelets[0], receiver_index, observed[0])
    if strips:
        return result
    return update_by_slabs(result, model_field, geometry, subs)


def solution(mesh):
    placed = (
        P(("grp", "sub"), None, None),
        P(("grp", "shot"), None),
        P(("grp", "shot"), None, None),
        P(("grp", "shot"), None),
        P(("grp", "shot"), None, None),
    )
    return jax.shard_map(
        per_device,
        mesh=mesh,
        in_specs=placed,
        out_specs=(P(("grp", "sub"), None, None), P(("grp", "sub"), "shot", None)),
        check_vma=False,
    )
```
